32 devices in a mesh: seq: 4 (over y, x), fsdp: 4 (over z), grp: 2 (over core).
Axes of the slice: x: 2, y: 2, z: 4, core: 2. Of those that a mesh axis runs over, the one named last changes fastest.
Arguments:
- queries: bfloat16 [1, 2048, 2048], P(None, ('seq', 'fsdp'), 'grp'), may hold values from -208 to 208
- encodings: bfloat16 [1, 32, 2, 128, 896], P(None, ('seq', 'fsdp'), None, 'grp'), may hold values from -6 to 6
- neighbour_lengths: int32 [1, 32, 2], P(None, ('seq', 'fsdp')), may hold values from 32 to 128
- key_weight: bfloat16 [896, 2048], P(None, 'grp'), may hold values from -0.1875 to 0.1875
- value_weight: bfloat16 [896, 2048], P(None, 'grp'), may hold values from -0.1875 to 0.1875
Outputs:
- attended: bfloat16 [1, 2048, 2048], P(None, ('seq', 'fsdp'), 'grp')
The draws below stay inside these ranges and needn't reach their ends.
All inputs are finite; a program needn't handle non-finite values.
Results may differ from the reference program's by a relative error of at most 0.011.
Values may be sent and summed in bfloat16 or wider, within the bound.
No kernel may reach another device: no remote copies, remote signals or barrier semaphores. Data moves between devices by JAX's collectives and lax.ppermute only.
A program may use at most 64 MiB of HBM per device.

```python
import jax
import jax.numpy as jnp
from jax import lax

HEADS = 16
HEAD_DIM = 128
ENC_WIDTH = 896
GROUP = 64
NEIGH = 2
NB_LEN = 128
SEQS = 1
N_GROUPS = 32
SEQ_LEN = 2048
ATT_WIDTH = 2048


def draw_queries(key, part):
    full_shape = (SEQS, SEQ_LEN, HEADS * HEAD_DIM)
    base_key = jax.random.fold_in(key, 0)
    values = jnp.clip(2.0 * jax.random.normal(base_key, full_shape, jnp.float32), -12.0, 12.0)
    return values.astype(jnp.bfloat16)


def set_ends(drawn, key, smallest, high):
    dims = drawn.shape
    index_at = [jax.random.randint(jax.random.fold_in(key, axis), (), 0, dims[axis]) for axis in range(len(dims))]
    drawn = drawn.at[tuple(index_at)].set(smallest)
    longest = dims.index(max(dims))
    index_at[longest] = (index_at[longest] + 1) % dims[longest]
    return drawn.at[tuple(index_at)].set(high)


def block_scale(rng, extent, shards, low, largest):
    loudness, own = 1.0, jax.random.fold_in(rng, 6)
    for dim, parts in shards:
        draws = jnp.exp(jax.random.uniform(jax.random.fold_in(own, dim), (parts,), jnp.float32, low / len(shards), largest / len(shards)))
        loudness = loudness * jnp.repeat(draws, extent[dim] // parts).reshape([-1 if axis == dim else 1 for axis in range(len(extent))])
    return loudness


def scatter_about(rng, shape, width, limit, cuts=(), held_as=jnp.bfloat16):
    array = width * jax.random.normal(rng, shape, jnp.float32)
    if cuts:
        array = array * block_scale(rng, shape, cuts, -0.22, 0.18)
    return jnp.clip(array, -limit, limit).astype(held_as)


def setup_inputs(seed: int = 0) -> dict:
    splits = jax.random.split(jax.random.key(seed), 6)
    return {
        "queries": draw_queries(jax.random.fold_in(splits[5], 71), 0),
        "encodings": scatter_about(splits[1], (SEQS, N_GROUPS, NEIGH, NB_LEN, ENC_WIDTH), 1.0, 6.0, ((1, 16), (3, 2))),
        "neighbour_lengths": set_ends(jax.random.randint(splits[2], (SEQS, N_GROUPS, NEIGH), NB_LEN // 4, NB_LEN + 1), jax.random.fold_in(splits[2], 1), NB_LEN // 4, NB_LEN).astype(jnp.int32),
        "key_weight": scatter_about(splits[3], (ENC_WIDTH, ATT_WIDTH), ENC_WIDTH ** -0.5, 0.1875, ((1, 2),)),
        "value_weight": scatter_about(splits[4], (ENC_WIDTH, ATT_WIDTH), ENC_WIDTH ** -0.5, 0.1875, ((1, 2),)),
    }


mask_fill = -1.0e30


def reference(queries, encodings, neighbour_lengths, key_weight, value_weight):
    total_cols = HEADS * HEAD_DIM
    softmax_scale = HEAD_DIM ** -0.5
    lead_zeros = jnp.zeros((SEQS, 1, total_cols), jnp.bfloat16)
    trail_zeros = jnp.zeros((SEQS, GROUP - 1, total_cols), jnp.bfloat16)
    padded = jnp.concatenate([lead_zeros, queries, trail_zeros], axis=1)
    padded = jnp.moveaxis(padded.reshape(SEQS, N_GROUPS + 1, GROUP, total_cols), 1, 0)

    def one_block(block_index):
        block_queries = lax.dynamic_index_in_dim(padded, block_index, 0, keepdims=False)
        source = jnp.maximum(block_index - 1, 0).astype(jnp.int32)
        enc_rows = lax.dynamic_index_in_dim(encodings, source, 1, keepdims=False)
        lengths = lax.dynamic_index_in_dim(neighbour_lengths, source, 1, keepdims=False)
        flat_rows = enc_rows.reshape(SEQS * NEIGH * NB_LEN, ENC_WIDTH)
        key_rows = jnp.dot(flat_rows, key_weight, preferred_element_type=jnp.float32).astype(jnp.bfloat16)
        value_rows = jnp.dot(flat_rows, value_weight, preferred_element_type=jnp.float32).astype(jnp.bfloat16)
        key_rows = key_rows.reshape(SEQS, NEIGH * NB_LEN, HEADS, HEAD_DIM)
        value_rows = value_rows.reshape(SEQS, NEIGH * NB_LEN, HEADS, HEAD_DIM)
        query_heads = block_queries.reshape(SEQS, GROUP, HEADS, HEAD_DIM)
        scores = jnp.einsum("bqhd,bkhd->bhqk", query_heads.astype(jnp.float32), key_rows.astype(jnp.float32)) * softmax_scale
        position = lax.broadcasted_iota(jnp.int32, (SEQS, NEIGH, NB_LEN), 2)
        key_live = (position < lengths[:, :, None]).reshape(SEQS, 1, 1, NEIGH * NB_LEN)
        scores = jnp.where(key_live, scores, mask_fill)
        row_max = jnp.max(scores, axis=-1, keepdims=True)
        weights = jnp.exp(scores - row_max)
        attention = (weights / jnp.sum(weights, axis=-1, keepdims=True)).astype(jnp.bfloat16)
        attended = jnp.einsum("bhqk,bkhd->bqhd", attention.astype(jnp.float32), value_rows.astype(jnp.float32))
        attended = attended.astype(jnp.bfloat16).reshape(SEQS, GROUP, total_cols)
        return jnp.where(block_index > 0, attended, jnp.zeros_like(attended))

    blocks = lax.map(one_block, jnp.arange(N_GROUPS + 1, dtype=jnp.int32))
    joined = jnp.moveaxis(blocks, 0, 1).reshape(SEQS, (N_GROUPS + 1) * GROUP, total_cols)
    return joined[:, 1:1 + SEQ_LEN]
```

```python
import math

import jax
import jax.numpy as jnp
from jax import lax
from jax.experimental import pallas as pl
from jax.experimental.pallas import tpu as pltpu
from jax.sharding import PartitionSpec as P

HEAD_DIM = 128
MASK_FILL = -1e30
SCORE_SCALE = HEAD_DIM ** (-0.5) * math.log2(math.e)
DEAD = 8.0
AXES = ("seq", "fsdp")


def dot(a, b):
    return jnp.dot(a, b, preferred_element_type=jnp.float32)


def dot_nt(a, b):
    return lax.dot_general(a, b, (((1,), (1,)), ((), ())), preferred_element_type=jnp.float32)


def softmax_weights(scores, dead):
    scores = jnp.where(dead, MASK_FILL, scores * SCORE_SCALE)
    return jnp.exp2(scores - jnp.max(scores, axis=-1, keepdims=True)).astype(jnp.bfloat16)


def mix(weights, rows):
    ones = jnp.ones((rows.shape[0], 128), jnp.bfloat16)
    mixed = dot(weights, jnp.concatenate([rows, ones], axis=1))
    return mixed[:, :-128] * (1.0 / mixed[:, -1:])


def payload_kernel(length_hbm, enc_hbm, out_ref, dead_ref, length_ref, sems):
    group_count, neighbours, nb_half, _ = enc_hbm.shape[1:]
    copies = [
        pltpu.make_async_copy(length_hbm, length_ref, sems.at[0]),
        pltpu.make_async_copy(enc_hbm.at[0, group_count - 1], out_ref, sems.at[1]),
    ]
    for copy in copies:
        copy.start()
    core = lax.axis_index("grp")
    key = lax.broadcasted_iota(jnp.int32, (1, 2 * neighbours * nb_half), 1)
    row = lax.broadcasted_iota(jnp.int32, (nb_half, 128), 0) + core * nb_half
    lane = lax.broadcasted_iota(jnp.int32, (nb_half, 128), 1)
    copies[0].wait()

    def length(g, n):
        return length_ref[0, g : g + 1, n : n + 1]

    for g in range(group_count):
        ends = [jnp.broadcast_to(length(g, n), key.shape) for n in range(neighbours)]
        dead = jnp.zeros(key.shape, jnp.int32)
        for block in range(2 * neighbours):
            place = key - block * nb_half
            here = (place >= 0) & (place < nb_half)
            dead = jnp.where(here & (place + block // neighbours * nb_half >= ends[block % neighbours]), 1, dead)
        dead_ref[pl.ds(g, 1), :] = dead
    marks = [
        (lane == 0) & (row >= jnp.broadcast_to(length(group_count - 1, n), row.shape)) for n in range(neighbours)
    ]
    copies[1].wait()
    for n in range(neighbours):
        part = out_ref[n, :, :128].astype(jnp.float32)
        out_ref[n, :, :128] = jnp.where(marks[n], DEAD, part).astype(jnp.bfloat16)


def local_kernel(dead_ref, query_ref, enc_ref, kw_ref, vw_ref, out_ref, map_ref):
    tok_count, col_count = query_ref.shape[1:]
    head_count = col_count // HEAD_DIM
    neighbours, nb_half, enc_width = enc_ref.shape[3:]
    half = neighbours * nb_half
    glen = tok_count // 2

    def group(g):
        rows = [enc_ref[core, 0, g].reshape(half, enc_width) for core in range(2)]
        return jnp.concatenate(rows, axis=0), dead_ref[g : g + 1, :] > 0

    query = pltpu.roll(query_ref[0].astype(jnp.float32), 1, 0).astype(jnp.bfloat16)

    head_row = lax.broadcasted_iota(jnp.int32, (16, 1), 0)
    row = lax.broadcasted_iota(jnp.int32, (glen, enc_width), 0)
    lane = lax.broadcasted_iota(jnp.int32, (1, enc_width), 1)
    one_hot = jnp.where(lane == 0, 1.0, 0.0)
    last = jnp.zeros((16, enc_width), jnp.float32)
    for h in range(head_count):
        cols = slice(h * HEAD_DIM, (h + 1) * HEAD_DIM)
        mapped = dot_nt(query[:glen, cols], kw_ref[:, cols])
        last = jnp.where(head_row == h, mapped[0:1], last)
        map_ref[pl.ds(h * glen, glen), :] = jnp.where(row == 0, one_hot, mapped).astype(jnp.bfloat16)

    enc, dead = group(1)
    last = mix(softmax_weights(dot_nt(last.astype(jnp.bfloat16), enc), dead), enc).astype(jnp.bfloat16)

    enc, dead = group(0)
    value_lhs = jnp.concatenate([enc, last], axis=0)
    wide = 2 * HEAD_DIM
    for c in range(col_count // wide):
        cols = slice(c * wide, (c + 1) * wide)
        keys = dot(enc, kw_ref[:, cols]).astype(jnp.bfloat16)
        values = dot(value_lhs, vw_ref[:, cols])
        last_out = values[2 * half :]
        values = values[: 2 * half].astype(jnp.bfloat16)
        for i in range(2):
            h = 2 * c + i
            cols = slice(h * HEAD_DIM, (h + 1) * HEAD_DIM)
            own = slice(i * HEAD_DIM, (i + 1) * HEAD_DIM)
            weights = softmax_weights(dot_nt(query[glen:, cols], keys[:, own]), dead)
            out = mix(weights, values[:, own])
            first = jnp.broadcast_to(last_out[h : h + 1, own], (glen, HEAD_DIM))
            out = pltpu.roll(jnp.concatenate([first, out], axis=0), tok_count - 1, 0)
            out_ref[:, cols] = out.astype(jnp.bfloat16)


def own_value_kernel(own_ref, vw_ref, value_ref):
    value_ref[...] = dot(own_ref[...].reshape(-1, own_ref.shape[-1]), vw_ref[...]).astype(jnp.bfloat16)


def halo_kernel(own_ref, other_ref, own_value_ref, map_ref, vw_ref, mid_ref, out_hbm, score_ref, top_ref, sems):
    tok_count, col_count = mid_ref.shape
    glen = tok_count // 2
    enc_width = own_ref.shape[-1]
    row = lax.broadcasted_iota(jnp.int32, (glen, 1), 0)
    is_first = lax.axis_index(AXES) == 0
    rest = pltpu.make_async_copy(mid_ref.at[pl.ds(glen, glen)], out_hbm.at[0, pl.ds(glen, glen)], sems.at[0])
    rest.start()

    @pl.when(is_first)
    def _():
        edge = mid_ref[:glen, :].astype(jnp.float32)
        top_ref[...] = jnp.where(row < glen - 1, 0.0, edge).astype(jnp.bfloat16)

    @pl.when(jnp.logical_not(is_first))
    def _():
        own, other = (ref[...].reshape(-1, enc_width) for ref in (own_ref, other_ref))
        score_ref[...] = dot_nt(map_ref[...], jnp.concatenate([own, other], axis=0))
        dead = score_ref[0:1, :] > DEAD - 1.0
        for start in range(0, col_count, 2 * HEAD_DIM):
            wide = slice(start, start + 2 * HEAD_DIM)
            other_value = dot(other, vw_ref[:, wide]).astype(jnp.bfloat16)
            value = jnp.concatenate([own_value_ref[:, wide], other_value], axis=0)
            for i in range(2):
                h = start // HEAD_DIM + i
                cols = slice(h * HEAD_DIM, (h + 1) * HEAD_DIM)
                weights = softmax_weights(score_ref[pl.ds(h * glen, glen), :], dead)
                out = mix(weights, value[:, i * HEAD_DIM : (i + 1) * HEAD_DIM])
                out = pltpu.roll(out, glen - 1, 0)
                out = jnp.where(row < glen - 1, out, mid_ref[:glen, cols].astype(jnp.float32))
                top_ref[:, cols] = out.astype(jnp.bfloat16)

    top = pltpu.make_async_copy(top_ref, out_hbm.at[0, pl.ds(0, glen)], sems.at[1])
    top.start()
    rest.wait()
    top.wait()


def shards(queries, encodings, neighbour_lengths, key_weight, value_weight):
    tok_count, col_count = queries.shape[1:]
    group_count, neighbours, nb_half, enc_width = encodings.shape[1:]
    key_count = 2 * neighbours * nb_half
    glen = tok_count // group_count
    rows = col_count // HEAD_DIM * glen
    vmem = pl.BlockSpec(memory_space=pltpu.VMEM)
    hbm = pl.BlockSpec(memory_space=pltpu.HBM)
    params = pltpu.CompilerParams(vmem_limit_bytes=24 * 2**20)

    payload, dead = pl.pallas_call(
        payload_kernel,
        out_shape=[
            jax.ShapeDtypeStruct((neighbours, nb_half, enc_width), jnp.bfloat16),
            jax.ShapeDtypeStruct((group_count, key_count), jnp.int32),
        ],
        in_specs=[hbm, hbm],
        out_specs=[vmem, vmem],
        scratch_shapes=[pltpu.VMEM(neighbour_lengths.shape, jnp.int32), pltpu.SemaphoreType.DMA((2,))],
        compiler_params=pltpu.CompilerParams(vmem_limit_bytes=4 * 2**20),
        cost_estimate=pl.CostEstimate(flops=10**10, bytes_accessed=2**20, transcendentals=0),
        name="payload",
    )(*(pltpu.with_memory_space_constraint(x, pltpu.HBM) for x in (neighbour_lengths, encodings)))
    size = lax.axis_size(AXES)
    halo = lax.ppermute(payload, AXES, [(i, (i + 1) % size) for i in range(size)])
    enc = lax.all_gather(encodings, "grp", axis=0)
    mid, mapped = pl.pallas_call(
        local_kernel,
        out_shape=[
            jax.ShapeDtypeStruct((tok_count, col_count), jnp.bfloat16),
            jax.ShapeDtypeStruct((rows, enc_width), jnp.bfloat16),
        ],
        in_specs=[vmem] * 5,
        out_specs=[vmem] * 2,
        compiler_params=params,
        cost_estimate=pl.CostEstimate(flops=2 * 10**9, bytes_accessed=6 * 2**20, transcendentals=0),
        name="local_groups",
    )(dead, queries, enc, key_weight, value_weight)

    halo, mid, mapped = lax.optimization_barrier((halo, mid, mapped))
    halo_other = lax.ppermute(halo, "grp", [(0, 1), (1, 0)])
    own_value = pl.pallas_call(
        own_value_kernel,
        out_shape=jax.ShapeDtypeStruct((neighbours * nb_half, col_count), jnp.bfloat16),
        in_specs=[vmem] * 2,
        out_specs=vmem,
        compiler_params=params,
        cost_estimate=pl.CostEstimate(flops=3 * 10**8, bytes_accessed=2**20, transcendentals=0),
        name="own_values",
    )(halo, value_weight)
    return pl.pallas_call(
        halo_kernel,
        out_shape=jax.ShapeDtypeStruct(queries.shape, jnp.bfloat16),
        in_specs=[vmem] * 6,
        out_specs=hbm,
        scratch_shapes=[
            pltpu.VMEM((rows, key_count), jnp.float32),
            pltpu.VMEM((glen, col_count), jnp.bfloat16),
            pltpu.SemaphoreType.DMA((2,)),
        ],
        compiler_params=params,
        cost_estimate=pl.CostEstimate(flops=10**9, bytes_accessed=4 * 2**20, transcendentals=0),
        name="previous_group",
    )(halo, halo_other, own_value, mapped, value_weight, mid)


def solution(mesh):
    placed = (
        P(None, AXES, "grp"),
        P(None, AXES, None, "grp", None),
        P(None, AXES, None),
        P(None, "grp"),
        P(None, "grp"),
    )
    return jax.shard_map(
        shards,
        mesh=mesh,
        in_specs=placed,
        out_specs=P(None, AXES, "grp"),
        check_vma=False,
    )
```

```python
import math

import jax
import jax.numpy as jnp
from jax import lax
from jax.experimental import pallas as pl
from jax.experimental.pallas import tpu as pltpu
from jax.sharding import PartitionSpec as P

HEAD_DIM = 128
MASK_FILL = -1e30
SCORE_SCALE = HEAD_DIM ** (-0.5) * math.log2(math.e)
DEAD = 8.0
AXES = ("seq", "fsdp")


def dot(a, b):
    return jnp.dot(a, b, preferred_element_type=jnp.float32)


def dot_nt(a, b):
    return lax.dot_general(a, b, (((1,), (1,)), ((), ())), preferred_element_type=jnp.float32)


def softmax_weights(scores, dead):
    scores = jnp.where(dead, MASK_FILL, scores)
    return jnp.exp2(scores - jnp.max(scores, axis=-1, keepdims=True)).astype(jnp.bfloat16)


def mix(weights, rows):
    ones = jnp.ones((rows.shape[0], 128), jnp.bfloat16)
    mixed = dot(weights, jnp.concatenate([rows, ones], axis=1))
    return mixed[:, :-128] * (1.0 / mixed[:, -1:])


def payload_kernel(length_hbm, enc_hbm, out_ref, length_ref, sems):
    group_count, neighbours, nb_half, _ = enc_hbm.shape[1:]
    copies = [
        pltpu.make_async_copy(length_hbm, length_ref, sems.at[0]),
        pltpu.make_async_copy(enc_hbm.at[0, group_count - 1], out_ref, sems.at[1]),
    ]
    for copy in copies:
        copy.start()
    row = lax.broadcasted_iota(jnp.int32, (nb_half, 128), 0) + lax.axis_index("grp") * nb_half
    lane = lax.broadcasted_iota(jnp.int32, (nb_half, 128), 1)
    copies[0].wait()
    marks = [(lane == 0) & (row >= length_ref[0, group_count - 1, n]) for n in range(neighbours)]
    copies[1].wait()
    for n in range(neighbours):
        part = out_ref[n, :, :128].astype(jnp.float32)
        out_ref[n, :, :128] = jnp.where(marks[n], DEAD, part).astype(jnp.bfloat16)


def local_kernel(length_ref, query_ref, enc_ref, kw_hbm, vw_hbm, out_ref, map_ref, vw_ref, kw_ref, sems):
    tok_count, col_count = query_ref.shape[1:]
    head_count = col_count // HEAD_DIM
    neighbours, nb_half, enc_width = enc_ref.shape[3:]
    half = neighbours * nb_half
    glen = tok_count // 2
    wide = 2 * HEAD_DIM
    copies = [
        [
            pltpu.make_async_copy(src.at[:, pl.ds(start, wide)], dst.at[:, pl.ds(start, wide)], sems.at[i, start // wide])
            for start in range(0, col_count, wide)
        ]
        for i, (src, dst) in enumerate([(kw_hbm, kw_ref), (vw_hbm, vw_ref)])
    ]
    for part in copies:
        for copy in part:
            copy.start()

    def group(g):
        rows = [enc_ref[core, 0, g].reshape(half, enc_width) for core in range(2)]
        key = lax.broadcasted_iota(jnp.int32, (1, 2 * half), 1)
        live = key < 0
        for block in range(2 * neighbours):
            first = block * nb_half
            length = jnp.broadcast_to(length_ref[0, g : g + 1, block % neighbours : block % neighbours + 1], key.shape)
            end = first + jnp.clip(length - block // neighbours * nb_half, 0, nb_half)
            live = live | ((key >= first) & (key < end))
        return jnp.concatenate(rows, axis=0), jnp.logical_not(live)

    query = query_ref[0].astype(jnp.float32)
    row = lax.broadcasted_iota(jnp.int32, (glen, 1), 0)
    halo_query = jnp.where(row < glen - 1, query[:glen], query[tok_count - 1 :]).astype(jnp.bfloat16)
    query = pltpu.roll(query, 1, 0)[glen:].astype(jnp.bfloat16)

    head_row = lax.broadcasted_iota(jnp.int32, (16, 1), 0)
    lane = lax.broadcasted_iota(jnp.int32, (1, enc_width), 1)
    one_hot = jnp.where(lane == 0, 1.0, 0.0)
    last = jnp.zeros((16, enc_width), jnp.float32)
    for h in range(head_count):
        cols = slice(h * HEAD_DIM, (h + 1) * HEAD_DIM)
        if h % 2 == 0:
            copies[0][h // 2].wait()
        mapped = dot_nt(halo_query[:, cols], kw_ref[:, cols]) * SCORE_SCALE
        last = jnp.where(head_row == h, mapped[glen - 1 :], last)
        map_ref[pl.ds(h * glen, glen), :] = jnp.where(row < glen - 1, mapped, one_hot).astype(jnp.bfloat16)

    enc, dead = group(1)
    last = mix(softmax_weights(dot_nt(last.astype(jnp.bfloat16), enc), dead), enc).astype(jnp.bfloat16)

    enc, dead = group(0)
    value_lhs = jnp.concatenate([enc, last], axis=0)
    for c in range(col_count // wide):
        cols = slice(c * wide, (c + 1) * wide)
        copies[1][c].wait()
        keys = dot(enc, kw_ref[:, cols]).astype(jnp.bfloat16)
        values = dot(value_lhs, vw_ref[:, cols])
        last_out = values[2 * half :]
        values = values[: 2 * half].astype(jnp.bfloat16)
        for i in range(2):
            h = 2 * c + i
            cols = slice(h * HEAD_DIM, (h + 1) * HEAD_DIM)
            own = slice(i * HEAD_DIM, (i + 1) * HEAD_DIM)
            weights = softmax_weights(dot_nt(query[:, cols], keys[:, own]) * SCORE_SCALE, dead)
            out = mix(weights, values[:, own])
            first = jnp.broadcast_to(last_out[h : h + 1, own], (glen, HEAD_DIM))
            out = pltpu.roll(jnp.concatenate([first, out], axis=0), tok_count - 1, 0)
            out_ref[:, cols] = out.astype(jnp.bfloat16)


def own_value_kernel(own_ref, vw_ref, value_ref):
    value_ref[...] = dot(own_ref[...].reshape(-1, own_ref.shape[-1]), vw_ref[...]).astype(jnp.bfloat16)


def halo_kernel(
    own_ref, other_ref, own_value_ref, map_ref, vw_ref, mid_ref, out_hbm, score_ref, max_ref, weight_ref, top_ref, sems
):
    tok_count, col_count = mid_ref.shape
    head_count = col_count // HEAD_DIM
    key_count = score_ref.shape[1]
    glen = tok_count // 2
    enc_width = own_ref.shape[-1]
    row = lax.broadcasted_iota(jnp.int32, (glen, 1), 0)
    is_first = lax.axis_index(AXES) == 0
    rest = pltpu.make_async_copy(mid_ref.at[pl.ds(glen, glen)], out_hbm.at[0, pl.ds(glen, glen)], sems.at[0])
    rest.start()

    @pl.when(is_first)
    def _():
        edge = mid_ref[:glen, :].astype(jnp.float32)
        top_ref[...] = jnp.where(row < glen - 1, 0.0, edge).astype(jnp.bfloat16)

    @pl.when(jnp.logical_not(is_first))
    def _():
        own, other = (ref[...].reshape(-1, enc_width) for ref in (own_ref, other_ref))
        score_ref[...] = dot_nt(map_ref[...], jnp.concatenate([own, other], axis=0))
        other_value = dot(other, vw_ref[...]).astype(jnp.bfloat16)
        dead = score_ref[glen - 1 : glen, :] > DEAD - 1.0
        blocks = [pl.ds(start, 32) for start in range(0, head_count * glen, 32)]
        for block in blocks:
            scores = jnp.where(dead, MASK_FILL, score_ref[block, :])
            max_ref[block, :] = jnp.broadcast_to(jnp.max(scores, axis=-1, keepdims=True), (32, 128))
        for block in blocks:
            top = max_ref[block, :]
            for start in range(0, key_count, 128):
                part = slice(start, start + 128)
                scores = jnp.where(dead[:, part], MASK_FILL, score_ref[block, part])
                weight_ref[block, part] = jnp.exp2(scores - top).astype(jnp.bfloat16)
        for h in range(head_count):
            cols = slice(h * HEAD_DIM, (h + 1) * HEAD_DIM)
            value = jnp.concatenate([own_value_ref[:, cols], other_value[:, cols]], axis=0)
            out = mix(weight_ref[pl.ds(h * glen, glen), :], value)
            out = jnp.where(row < glen - 1, out, mid_ref[:glen, cols].astype(jnp.float32))
            top_ref[:, cols] = out.astype(jnp.bfloat16)

    top = pltpu.make_async_copy(top_ref, out_hbm.at[0, pl.ds(0, glen)], sems.at[1])
    top.start()
    rest.wait()
    top.wait()


def shards(queries, encodings, neighbour_lengths, key_weight, value_weight):
    tok_count, col_count = queries.shape[1:]
    group_count, neighbours, nb_half, enc_width = encodings.shape[1:]
    key_count = 2 * neighbours * nb_half
    glen = tok_count // group_count
    rows = col_count // HEAD_DIM * glen
    vmem = pl.BlockSpec(memory_space=pltpu.VMEM)
    hbm = pl.BlockSpec(memory_space=pltpu.HBM)
    params = pltpu.CompilerParams(vmem_limit_bytes=24 * 2**20)

    payload = pl.pallas_call(
        payload_kernel,
        out_shape=jax.ShapeDtypeStruct((neighbours, nb_half, enc_width), jnp.bfloat16),
        in_specs=[hbm, hbm],
        out_specs=vmem,
        scratch_shapes=[pltpu.SMEM(neighbour_lengths.shape, jnp.int32), pltpu.SemaphoreType.DMA((2,))],
        compiler_params=pltpu.CompilerParams(vmem_limit_bytes=4 * 2**20),
        cost_estimate=pl.CostEstimate(flops=10**10, bytes_accessed=2**20, transcendentals=0),
        name="payload",
    )(*(pltpu.with_memory_space_constraint(x, pltpu.HBM) for x in (neighbour_lengths, encodings)))
    size = lax.axis_size(AXES)
    halo = lax.ppermute(payload, AXES, [(i, (i + 1) % size) for i in range(size)])
    enc = lax.all_gather(encodings, "grp", axis=0)
    key_weight, value_weight = (pltpu.with_memory_space_constraint(x, pltpu.HBM) for x in (key_weight, value_weight))
    mid, mapped, value_weight = pl.pallas_call(
        local_kernel,
        out_shape=[
            jax.ShapeDtypeStruct((tok_count, col_count), jnp.bfloat16),
            jax.ShapeDtypeStruct((rows, enc_width), jnp.bfloat16),
            jax.ShapeDtypeStruct(value_weight.shape, jnp.bfloat16),
        ],
        in_specs=[vmem] * 3 + [hbm] * 2,
        out_specs=[vmem] * 3,
        scratch_shapes=[
            pltpu.VMEM(key_weight.shape, jnp.bfloat16),
            pltpu.SemaphoreType.DMA((2, col_count // (2 * HEAD_DIM))),
        ],
        compiler_params=params,
        cost_estimate=pl.CostEstimate(flops=2 * 10**9, bytes_accessed=6 * 2**20, transcendentals=0),
        name="local_groups",
    )(neighbour_lengths, queries, enc, key_weight, value_weight)

    halo, mid, mapped = lax.optimization_barrier((halo, mid, mapped))
    halo_other = lax.ppermute(halo, "grp", [(0, 1), (1, 0)])
    own_value = pl.pallas_call(
        own_value_kernel,
        out_shape=jax.ShapeDtypeStruct((neighbours * nb_half, col_count), jnp.bfloat16),
        in_specs=[vmem] * 2,
        out_specs=vmem,
        compiler_params=params,
        cost_estimate=pl.CostEstimate(flops=3 * 10**8, bytes_accessed=2**20, transcendentals=0),
        name="own_values",
    )(halo, value_weight)
    return pl.pallas_call(
        halo_kernel,
        out_shape=jax.ShapeDtypeStruct(queries.shape, jnp.bfloat16),
        in_specs=[vmem] * 6,
        out_specs=hbm,
        scratch_shapes=[
            pltpu.VMEM((rows, key_count), jnp.float32),
            pltpu.VMEM((rows, 128), jnp.float32),
            pltpu.VMEM((rows, key_count), jnp.bfloat16),
            pltpu.VMEM((glen, col_count), jnp.bfloat16),
            pltpu.SemaphoreType.DMA((2,)),
        ],
        compiler_params=params,
        cost_estimate=pl.CostEstimate(flops=10**9, bytes_accessed=4 * 2**20, transcendentals=0),
        name="previous_group",
    )(halo, halo_other, own_value, mapped, value_weight, mid)


def solution(mesh):
    placed = (
        P(None, AXES, "grp"),
        P(None, AXES, None, "grp", None),
        P(None, AXES, None),
        P(None, "grp"),
        P(None, "grp"),
    )
    return jax.shard_map(
        shards,
        mesh=mesh,
        in_specs=placed,
        out_specs=P(None, AXES, "grp"),
        check_vma=False,
    )
```

```python
import functools
import math

import jax
import jax.numpy as jnp
from jax import lax
from jax.experimental import pallas as pl
from jax.experimental.pallas import tpu as pltpu
from jax.sharding import PartitionSpec as P

HEAD_DIM = 128
MASK_FILL = -1e30
SCORE_SCALE = HEAD_DIM ** (-0.5) * math.log2(math.e)
DEAD = 8.0
AXES = ("seq", "fsdp")


def dot(a, b):
    return jnp.dot(a, b, preferred_element_type=jnp.float32)


def dot_nt(a, b):
    return lax.dot_general(a, b, (((1,), (1,)), ((), ())), preferred_element_type=jnp.float32)


def softmax_weights(scores, dead):
    scores = jnp.where(dead, MASK_FILL, scores)
    return jnp.exp2(scores - jnp.max(scores, axis=-1, keepdims=True)).astype(jnp.bfloat16)


def mix(weights, rows):
    ones = jnp.ones((rows.shape[0], 128), jnp.bfloat16)
    mixed = dot(weights, jnp.concatenate([rows, ones], axis=1))
    return mixed[:, :-128] * (1.0 / mixed[:, -1:])


def payload_kernel(length_hbm, enc_hbm, out_ref, length_ref, sems):
    group_count, neighbours, nb_half, _ = enc_hbm.shape[1:]
    quarters = [(n, pl.ds(i * nb_half // 2, nb_half // 2)) for n in range(neighbours) for i in range(2)]
    copies = [
        pltpu.make_async_copy(enc_hbm.at[0, group_count - 1].at[part], out_ref.at[part], sems.at[i])
        for i, part in enumerate(quarters)
    ]
    lengths = pltpu.make_async_copy(length_hbm, length_ref, sems.at[len(copies)])
    lengths.start()
    for copy in copies:
        copy.start()
    row = lax.broadcasted_iota(jnp.int32, (nb_half, 128), 0) + lax.axis_index("grp") * nb_half
    lane = lax.broadcasted_iota(jnp.int32, (nb_half, 128), 1)
    lengths.wait()
    marks = [(lane == 0) & (row >= length_ref[0, group_count - 1, n]) for n in range(neighbours)]
    for copy in copies:
        copy.wait()
    for n in range(neighbours):
        part = out_ref[n, :, :128].astype(jnp.float32)
        out_ref[n, :, :128] = jnp.where(marks[n], DEAD, part).astype(jnp.bfloat16)


def local_kernel(
    length_ref, query_ref, enc_ref, kw_hbm, vw_hbm, out_hbm, edge_ref, map_ref, vw_ref,
    kw_ref, key_ref, value_ref, score_ref, max_ref, weight_ref, out_ref, sems,
):
    tok_count, col_count = query_ref.shape[1:]
    head_count = col_count // HEAD_DIM
    neighbours, nb_half, enc_width = enc_ref.shape[3:]
    half = neighbours * nb_half
    glen = tok_count // 2
    heads = [slice(start, start + HEAD_DIM) for start in range(0, col_count, HEAD_DIM)]

    parts = sems.shape[1]
    depth = enc_width // parts
    copies = [
        [
            pltpu.make_async_copy(src.at[pl.ds(i * depth, depth)], dst.at[pl.ds(i * depth, depth)], sems.at[j, i])
            for i in range(parts)
        ]
        for j, (src, dst) in enumerate([(kw_hbm, kw_ref), (vw_hbm, vw_ref)])
    ]
    for weight_copies in copies:
        for copy in weight_copies:
            copy.start()

    def group(g):
        rows = [enc_ref[core, 0, g].reshape(half, enc_width) for core in range(2)]
        key = lax.broadcasted_iota(jnp.int32, (1, 2 * half), 1)
        live = key < 0
        for block in range(2 * neighbours):
            first = block * nb_half
            length = jnp.broadcast_to(length_ref[0, g : g + 1, block % neighbours : block % neighbours + 1], key.shape)
            end = first + jnp.clip(length - block // neighbours * nb_half, 0, nb_half)
            live = live | ((key >= first) & (key < end))
        return jnp.concatenate(rows, axis=0), jnp.logical_not(live)

    query = query_ref[0].astype(jnp.float32)
    row = lax.broadcasted_iota(jnp.int32, (glen, 1), 0)
    halo_query = jnp.where(row < glen - 1, query[:glen], query[tok_count - 1 :]).astype(jnp.bfloat16)
    query = pltpu.roll(query, 1, 0)[glen:].astype(jnp.bfloat16)

    enc, dead = group(0)
    for copy in copies[0]:
        copy.wait()
    key_ref[...] = dot(enc, kw_ref[...]).astype(jnp.bfloat16)

    head_row = lax.broadcasted_iota(jnp.int32, (16, 1), 0)
    lane = lax.broadcasted_iota(jnp.int32, (1, enc_width), 1)
    one_hot = jnp.where(lane == 0, 1.0, 0.0)
    last = jnp.zeros((16, enc_width), jnp.float32)
    for h, cols in enumerate(heads):
        mapped = dot_nt(halo_query[:, cols], kw_ref[:, cols]) * SCORE_SCALE
        last = jnp.where(head_row == h, mapped[glen - 1 :], last)
        map_ref[pl.ds(h * glen, glen), :] = jnp.where(row < glen - 1, mapped, one_hot).astype(jnp.bfloat16)
    for h, cols in enumerate(heads):
        score_ref[pl.ds(h * glen, glen), :] = dot_nt(query[:, cols], key_ref[:, cols]) * SCORE_SCALE

    last_enc, last_dead = group(1)
    last_weights = softmax_weights(dot_nt(last.astype(jnp.bfloat16), last_enc), last_dead)
    last = mix(last_weights, last_enc).astype(jnp.bfloat16)

    blocks = [pl.ds(start, 32) for start in range(0, head_count * glen, 32)]
    for block in blocks:
        scores = jnp.where(dead, MASK_FILL, score_ref[block, :])
        max_ref[block, :] = jnp.broadcast_to(jnp.max(scores, axis=-1, keepdims=True), (32, 128))
    for block in blocks:
        top = max_ref[block, :]
        for start in range(0, 2 * half, 128):
            part = slice(start, start + 128)
            scores = jnp.where(dead[:, part], MASK_FILL, score_ref[block, part])
            weight_ref[block, part] = jnp.exp2(scores - top).astype(jnp.bfloat16)

    for copy in copies[1]:
        copy.wait()
    values = dot(jnp.concatenate([enc, last], axis=0), vw_ref[...])
    value_ref[...] = values[: 2 * half].astype(jnp.bfloat16)
    last_out = values[2 * half :]
    token = lax.broadcasted_iota(jnp.int32, (tok_count, 1), 0)
    for h, cols in enumerate(heads):
        out = mix(weight_ref[pl.ds(h * glen, glen), :], value_ref[:, cols])
        first = jnp.broadcast_to(last_out[h : h + 1, cols], (glen, HEAD_DIM))
        out = pltpu.roll(jnp.concatenate([first, out], axis=0), tok_count - 1, 0)
        edge_ref[:, cols] = out[glen - 1 : glen]
        out_ref[:, cols] = jnp.where(token < glen - 1, 0.0, out).astype(jnp.bfloat16)
    copy = pltpu.make_async_copy(out_ref, out_hbm.at[0], sems.at[0, 0])
    copy.start()
    copy.wait()


def own_kernel(glen, own_ref, map_ref, vw_ref, value_ref, score_ref, max_ref):
    own = own_ref[...].reshape(-1, own_ref.shape[-1])
    value_ref[...] = dot(own, vw_ref[...]).astype(jnp.bfloat16)
    score_ref[...] = dot_nt(map_ref[...], own)
    dead = score_ref[glen - 1 : glen, :] > DEAD - 1.0
    for start in range(0, score_ref.shape[0], 32):
        block = pl.ds(start, 32)
        scores = jnp.where(dead, MASK_FILL, score_ref[block, :])
        score_ref[block, :] = scores
        max_ref[block, :] = jnp.broadcast_to(jnp.max(scores, axis=-1, keepdims=True), scores.shape)


def halo_kernel(
    other_ref, own_value_ref, own_score_ref, own_max_ref, map_ref, vw_ref, edge_ref, _, out_hbm,
    score_ref, max_ref, weight_ref, top_ref, sem,
):
    glen, col_count = top_ref.shape
    row_count, half = score_ref.shape

    @pl.when(lax.axis_index(AXES) > 0)
    def _():
        other = other_ref[...].reshape(half, -1)
        score_ref[...] = dot_nt(map_ref[...], other)
        other_value = dot(other, vw_ref[...]).astype(jnp.bfloat16)
        dead = score_ref[glen - 1 : glen, :] > DEAD - 1.0
        blocks = [pl.ds(start, 32) for start in range(0, row_count, 32)]
        for block in blocks:
            scores = jnp.where(dead, MASK_FILL, score_ref[block, :])
            own_max = own_max_ref[block, :]
            max_ref[block, :] = jnp.maximum(own_max, jnp.max(scores, axis=-1, keepdims=True))
        for block in blocks:
            top = max_ref[block, :]
            weight_ref[block, :half] = jnp.exp2(own_score_ref[block, :] - top).astype(jnp.bfloat16)
            scores = jnp.where(dead, MASK_FILL, score_ref[block, :])
            weight_ref[block, half:] = jnp.exp2(scores - top).astype(jnp.bfloat16)
        row = lax.broadcasted_iota(jnp.int32, (glen, 1), 0)
        for start in range(0, col_count, HEAD_DIM):
            cols = slice(start, start + HEAD_DIM)
            value = jnp.concatenate([own_value_ref[:, cols], other_value[:, cols]], axis=0)
            out = mix(weight_ref[pl.ds(start // HEAD_DIM * glen, glen), :], value)
            top_ref[:, cols] = jnp.where(row < glen - 1, out, edge_ref[:, cols]).astype(jnp.bfloat16)
        copy = pltpu.make_async_copy(top_ref, out_hbm.at[0, pl.ds(0, glen)], sem)
        copy.start()
        copy.wait()


def shards(queries, encodings, neighbour_lengths, key_weight, value_weight):
    tok_count, col_count = queries.shape[1:]
    group_count, neighbours, nb_half, enc_width = encodings.shape[1:]
    half = neighbours * nb_half
    glen = tok_count // group_count
    rows = col_count // HEAD_DIM * glen
    vmem = pl.BlockSpec(memory_space=pltpu.VMEM)
    hbm = pl.BlockSpec(memory_space=pltpu.HBM)
    params = pltpu.CompilerParams(vmem_limit_bytes=24 * 2**20)

    payload = pl.pallas_call(
        payload_kernel,
        out_shape=jax.ShapeDtypeStruct((neighbours, nb_half, enc_width), jnp.bfloat16),
        in_specs=[hbm, hbm],
        out_specs=vmem,
        scratch_shapes=[pltpu.SMEM(neighbour_lengths.shape, jnp.int32), pltpu.SemaphoreType.DMA((2 * neighbours + 1,))],
        compiler_params=pltpu.CompilerParams(vmem_limit_bytes=4 * 2**20),
        cost_estimate=pl.CostEstimate(flops=10**10, bytes_accessed=2**20, transcendentals=0),
        name="payload",
    )(*(pltpu.with_memory_space_constraint(x, pltpu.HBM) for x in (neighbour_lengths, encodings)))
    size = lax.axis_size(AXES)
    halo = lax.ppermute(payload, AXES, [(i, (i + 1) % size) for i in range(size)])
    enc = lax.all_gather(encodings, "grp", axis=0)
    key_weight, value_weight = (pltpu.with_memory_space_constraint(x, pltpu.HBM) for x in (key_weight, value_weight))
    out, edge, mapped, value_weight = pl.pallas_call(
        local_kernel,
        out_shape=[
            jax.ShapeDtypeStruct(queries.shape, jnp.bfloat16),
            jax.ShapeDtypeStruct((1, col_count), jnp.float32),
            jax.ShapeDtypeStruct((rows, enc_width), jnp.bfloat16),
            jax.ShapeDtypeStruct(value_weight.shape, jnp.bfloat16),
        ],
        in_specs=[vmem] * 3 + [hbm] * 2,
        out_specs=[hbm] + [vmem] * 3,
        scratch_shapes=[
            pltpu.VMEM(key_weight.shape, jnp.bfloat16),
            pltpu.VMEM((2 * half, col_count), jnp.bfloat16),
            pltpu.VMEM((2 * half, col_count), jnp.bfloat16),
            pltpu.VMEM((rows, 2 * half), jnp.float32),
            pltpu.VMEM((rows, 128), jnp.float32),
            pltpu.VMEM((rows, 2 * half), jnp.bfloat16),
            pltpu.VMEM((tok_count, col_count), jnp.bfloat16),
            pltpu.SemaphoreType.DMA((2, 4)),
        ],
        compiler_params=params,
        cost_estimate=pl.CostEstimate(flops=2 * 10**9, bytes_accessed=6 * 2**20, transcendentals=0),
        name="local_groups",
    )(neighbour_lengths, queries, enc, key_weight, value_weight)

    halo, out, mapped = lax.optimization_barrier((halo, out, mapped))
    halo_other = lax.ppermute(halo, "grp", [(0, 1), (1, 0)])
    own_value, own_score, own_max = pl.pallas_call(
        functools.partial(own_kernel, glen),
        out_shape=[
            jax.ShapeDtypeStruct((half, col_count), jnp.bfloat16),
            jax.ShapeDtypeStruct((rows, half), jnp.float32),
            jax.ShapeDtypeStruct((rows, half), jnp.float32),
        ],
        in_specs=[vmem] * 3,
        out_specs=[vmem] * 3,
        compiler_params=params,
        cost_estimate=pl.CostEstimate(flops=3 * 10**8, bytes_accessed=2**20, transcendentals=0),
        name="own_half",
    )(halo, mapped, value_weight)
    return pl.pallas_call(
        halo_kernel,
        out_shape=jax.ShapeDtypeStruct(queries.shape, jnp.bfloat16),
        in_specs=[vmem] * 7 + [hbm],
        out_specs=hbm,
        scratch_shapes=[
            pltpu.VMEM((rows, half), jnp.float32),
            pltpu.VMEM((rows, half), jnp.float32),
            pltpu.VMEM((rows, 2 * half), jnp.bfloat16),
            pltpu.VMEM((glen, col_count), jnp.bfloat16),
            pltpu.SemaphoreType.DMA,
        ],
        input_output_aliases={7: 0},
        compiler_params=params,
        cost_estimate=pl.CostEstimate(flops=10**9, bytes_accessed=4 * 2**20, transcendentals=0),
        name="previous_group",
    )(
        halo_other, own_value, own_score, own_max, mapped, value_weight, edge,
        pltpu.with_memory_space_constraint(out, pltpu.HBM),
    )


def solution(mesh):
    placed = (
        P(None, AXES, "grp"),
        P(None, AXES, None, "grp", None),
        P(None, AXES, None),
        P(None, "grp"),
        P(None, "grp"),
    )
    return jax.shard_map(
        shards,
        mesh=mesh,
        in_specs=placed,
        out_specs=P(None, AXES, "grp"),
        check_vma=False,
    )
```

```python
import functools
import math

import jax
import jax.numpy as jnp
from jax import lax
from jax.experimental import pallas as pl
from jax.experimental.pallas import tpu as pltpu
from jax.sharding import PartitionSpec as P

HEAD_DIM = 128
MASK_FILL = -1e30
SCORE_SCALE = HEAD_DIM ** (-0.5) * math.log2(math.e)
DEAD = 8.0
AXES = ("seq", "fsdp")


def dot(a, b):
    return jnp.dot(a, b, preferred_element_type=jnp.float32)


def dot_nt(a, b):
    return lax.dot_general(a, b, (((1,), (1,)), ((), ())), preferred_element_type=jnp.float32)


def softmax_weights(scores, dead):
    scores = jnp.where(dead, MASK_FILL, scores)
    return jnp.exp2(scores - jnp.max(scores, axis=-1, keepdims=True)).astype(jnp.bfloat16)


def mix(weights, rows):
    ones = jnp.ones((rows.shape[0], 128), jnp.bfloat16)
    mixed = dot(weights, jnp.concatenate([rows, ones], axis=1))
    return mixed[:, :-128] * (1.0 / mixed[:, -1:])


def payload_kernel(length_hbm, enc_hbm, out_ref, length_ref, sems):
    group_count, neighbours, nb_half, _ = enc_hbm.shape[1:]
    rows = [pl.ds(n * nb_half, nb_half) for n in range(neighbours)]
    copies = [
        pltpu.make_async_copy(enc_hbm.at[0, group_count - 1, n], out_ref.at[rows[n]], sems.at[n])
        for n in range(neighbours)
    ]
    lengths = pltpu.make_async_copy(length_hbm, length_ref, sems.at[len(copies)])
    lengths.start()
    for copy in copies:
        copy.start()
    row = lax.broadcasted_iota(jnp.int32, (nb_half, 128), 0) + lax.axis_index("grp") * nb_half
    lane = lax.broadcasted_iota(jnp.int32, (nb_half, 128), 1)
    lengths.wait()
    marks = [(lane == 0) & (row >= length_ref[0, group_count - 1, n]) for n in range(neighbours)]
    for copy in copies:
        copy.wait()
    for n in range(neighbours):
        part = out_ref[rows[n], :128].astype(jnp.float32)
        out_ref[rows[n], :128] = jnp.where(marks[n], DEAD, part).astype(jnp.bfloat16)


def local_kernel(
    length_ref, enc_ref, query_hbm, kw_hbm, vw_hbm, out_hbm, edge_ref, map_ref, vw_ref,
    query_ref, kw_ref, key_ref, value_ref, score_ref, max_ref, weight_ref, out_ref, sems,
):
    tok_count, col_count = query_ref.shape
    head_count = col_count // HEAD_DIM
    neighbours, nb_half, enc_width = enc_ref.shape[3:]
    half = neighbours * nb_half
    glen = tok_count // 2
    heads = [slice(start, start + HEAD_DIM) for start in range(0, col_count, HEAD_DIM)]

    parts = sems.shape[1] - 1
    query_copy = pltpu.make_async_copy(query_hbm.at[0], query_ref, sems.at[0, parts])
    query_copy.start()
    depth = enc_width // parts
    copies = [
        [
            pltpu.make_async_copy(src.at[pl.ds(i * depth, depth)], dst.at[pl.ds(i * depth, depth)], sems.at[j, i])
            for i in range(parts)
        ]
        for j, (src, dst) in enumerate([(kw_hbm, kw_ref), (vw_hbm, vw_ref)])
    ]
    for weight_copies in copies:
        for copy in weight_copies:
            copy.start()

    def group(g):
        rows = [enc_ref[core, 0, g].reshape(half, enc_width) for core in range(2)]
        key = lax.broadcasted_iota(jnp.int32, (1, 2 * half), 1)
        live = key < 0
        for block in range(2 * neighbours):
            first = block * nb_half
            length = jnp.broadcast_to(length_ref[0, g : g + 1, block % neighbours : block % neighbours + 1], key.shape)
            end = first + jnp.clip(length - block // neighbours * nb_half, 0, nb_half)
            live = live | ((key >= first) & (key < end))
        return jnp.concatenate(rows, axis=0), jnp.logical_not(live)

    query_copy.wait()
    query = query_ref[...].astype(jnp.float32)
    row = lax.broadcasted_iota(jnp.int32, (glen, 1), 0)
    halo_query = jnp.where(row < glen - 1, query[:glen], query[tok_count - 1 :]).astype(jnp.bfloat16)
    query = pltpu.roll(query, 1, 0)[glen:].astype(jnp.bfloat16)

    enc, dead = group(0)
    for copy in copies[0]:
        copy.wait()
    key_ref[...] = dot(enc, kw_ref[...]).astype(jnp.bfloat16)

    head_row = lax.broadcasted_iota(jnp.int32, (16, 1), 0)
    lane = lax.broadcasted_iota(jnp.int32, (1, enc_width), 1)
    one_hot = jnp.where(lane == 0, 1.0, 0.0)
    last = jnp.zeros((16, enc_width), jnp.float32)
    for h, cols in enumerate(heads):
        mapped = dot_nt(halo_query[:, cols], kw_ref[:, cols]) * SCORE_SCALE
        last = jnp.where(head_row == h, mapped[glen - 1 :], last)
        map_ref[pl.ds(h * glen, glen), :] = jnp.where(row < glen - 1, mapped, one_hot).astype(jnp.bfloat16)
    for h, cols in enumerate(heads):
        score_ref[pl.ds(h * glen, glen), :] = dot_nt(query[:, cols], key_ref[:, cols]) * SCORE_SCALE

    last_enc, last_dead = group(1)
    last_weights = softmax_weights(dot_nt(last.astype(jnp.bfloat16), last_enc), last_dead)
    last = mix(last_weights, last_enc).astype(jnp.bfloat16)

    blocks = [pl.ds(start, 32) for start in range(0, head_count * glen, 32)]
    for block in blocks:
        scores = jnp.where(dead, MASK_FILL, score_ref[block, :])
        max_ref[block, :] = jnp.broadcast_to(jnp.max(scores, axis=-1, keepdims=True), (32, 128))
    for block in blocks:
        top = max_ref[block, :]
        for start in range(0, 2 * half, 128):
            part = slice(start, start + 128)
            scores = jnp.where(dead[:, part], MASK_FILL, score_ref[block, part])
            weight_ref[block, part] = jnp.exp2(scores - top).astype(jnp.bfloat16)

    for copy in copies[1]:
        copy.wait()
    values = dot(jnp.concatenate([enc, last], axis=0), vw_ref[...])
    value_ref[...] = values[: 2 * half].astype(jnp.bfloat16)
    last_out = values[2 * half :]
    token = lax.broadcasted_iota(jnp.int32, (tok_count, 1), 0)
    for h, cols in enumerate(heads):
        out = mix(weight_ref[pl.ds(h * glen, glen), :], value_ref[:, cols])
        first = jnp.broadcast_to(last_out[h : h + 1, cols], (glen, HEAD_DIM))
        out = pltpu.roll(jnp.concatenate([first, out], axis=0), tok_count - 1, 0)
        edge_ref[:, cols] = out[glen - 1 : glen]
        out_ref[:, cols] = jnp.where(token < glen - 1, 0.0, out).astype(jnp.bfloat16)
    copy = pltpu.make_async_copy(out_ref, out_hbm.at[0], sems.at[0, 0])
    copy.start()
    copy.wait()


def own_kernel(glen, own_ref, map_ref, vw_ref, value_ref, score_ref, max_ref):
    own = own_ref[...]
    value_ref[...] = dot(own, vw_ref[...]).astype(jnp.bfloat16)
    score_ref[...] = dot_nt(map_ref[...], own)
    dead = score_ref[glen - 1 : glen, :] > DEAD - 1.0
    for start in range(0, score_ref.shape[0], 32):
        block = pl.ds(start, 32)
        scores = jnp.where(dead, MASK_FILL, score_ref[block, :])
        score_ref[block, :] = scores
        max_ref[block, :] = jnp.broadcast_to(jnp.max(scores, axis=-1, keepdims=True), scores.shape)


def halo_kernel(
    other_ref, own_value_ref, own_score_ref, own_max_ref, map_ref, vw_ref, edge_ref, _, out_hbm,
    score_ref, max_ref, weight_ref, top_ref, sem,
):
    glen, col_count = top_ref.shape
    row_count, half = score_ref.shape

    @pl.when(lax.axis_index(AXES) > 0)
    def _():
        other = other_ref[...]
        score_ref[...] = dot_nt(map_ref[...], other)
        other_value = dot(other, vw_ref[...]).astype(jnp.bfloat16)
        dead = score_ref[glen - 1 : glen, :] > DEAD - 1.0
        blocks = [pl.ds(start, 32) for start in range(0, row_count, 32)]
        for block in blocks:
            scores = jnp.where(dead, MASK_FILL, score_ref[block, :])
            own_max = own_max_ref[block, :]
            max_ref[block, :] = jnp.maximum(own_max, jnp.max(scores, axis=-1, keepdims=True))
        for block in blocks:
            top = max_ref[block, :]
            weight_ref[block, :half] = jnp.exp2(own_score_ref[block, :] - top).astype(jnp.bfloat16)
            scores = jnp.where(dead, MASK_FILL, score_ref[block, :])
            weight_ref[block, half:] = jnp.exp2(scores - top).astype(jnp.bfloat16)
        row = lax.broadcasted_iota(jnp.int32, (glen, 1), 0)
        for start in range(0, col_count, HEAD_DIM):
            cols = slice(start, start + HEAD_DIM)
            value = jnp.concatenate([own_value_ref[:, cols], other_value[:, cols]], axis=0)
            out = mix(weight_ref[pl.ds(start // HEAD_DIM * glen, glen), :], value)
            top_ref[:, cols] = jnp.where(row < glen - 1, out, edge_ref[:, cols]).astype(jnp.bfloat16)
        copy = pltpu.make_async_copy(top_ref, out_hbm.at[0, pl.ds(0, glen)], sem)
        copy.start()
        copy.wait()


def shards(queries, encodings, neighbour_lengths, key_weight, value_weight):
    tok_count, col_count = queries.shape[1:]
    group_count, neighbours, nb_half, enc_width = encodings.shape[1:]
    half = neighbours * nb_half
    glen = tok_count // group_count
    rows = col_count // HEAD_DIM * glen
    vmem = pl.BlockSpec(memory_space=pltpu.VMEM)
    hbm = pl.BlockSpec(memory_space=pltpu.HBM)
    params = pltpu.CompilerParams(vmem_limit_bytes=24 * 2**20)

    payload = pl.pallas_call(
        payload_kernel,
        out_shape=pltpu.VMEM((half, enc_width), jnp.bfloat16),
        in_specs=[hbm, hbm],
        out_specs=vmem,
        scratch_shapes=[pltpu.SMEM(neighbour_lengths.shape, jnp.int32), pltpu.SemaphoreType.DMA((neighbours + 1,))],
        compiler_params=pltpu.CompilerParams(vmem_limit_bytes=127 * 2**19),
        cost_estimate=pl.CostEstimate(flops=10**10, bytes_accessed=2**20, transcendentals=0),
        name="payload",
    )(*(pltpu.with_memory_space_constraint(x, pltpu.HBM) for x in (neighbour_lengths, encodings)))
    size = lax.axis_size(AXES)
    halo = lax.ppermute(payload, AXES, [(i, (i + 1) % size) for i in range(size)])
    enc = lax.all_gather(encodings, "grp", axis=0)
    fetched = (pltpu.with_memory_space_constraint(x, pltpu.HBM) for x in (queries, key_weight, value_weight))
    out, edge, mapped, value_weight = pl.pallas_call(
        local_kernel,
        out_shape=[
            jax.ShapeDtypeStruct(queries.shape, jnp.bfloat16),
            jax.ShapeDtypeStruct((1, col_count), jnp.float32),
            jax.ShapeDtypeStruct((rows, enc_width), jnp.bfloat16),
            jax.ShapeDtypeStruct(value_weight.shape, jnp.bfloat16),
        ],
        in_specs=[vmem] * 2 + [hbm] * 3,
        out_specs=[hbm] + [vmem] * 3,
        scratch_shapes=[
            pltpu.VMEM((tok_count, col_count), jnp.bfloat16),
            pltpu.VMEM(key_weight.shape, jnp.bfloat16),
            pltpu.VMEM((2 * half, col_count), jnp.bfloat16),
            pltpu.VMEM((2 * half, col_count), jnp.bfloat16),
            pltpu.VMEM((rows, 2 * half), jnp.float32),
            pltpu.VMEM((rows, 128), jnp.float32),
            pltpu.VMEM((rows, 2 * half), jnp.bfloat16),
            pltpu.VMEM((tok_count, col_count), jnp.bfloat16),
            pltpu.SemaphoreType.DMA((2, 5)),
        ],
        compiler_params=params,
        cost_estimate=pl.CostEstimate(flops=2 * 10**9, bytes_accessed=6 * 2**20, transcendentals=0),
        name="local_groups",
    )(neighbour_lengths, enc, *fetched)

    halo, out, mapped = lax.optimization_barrier((halo, out, mapped))
    halo_other = lax.ppermute(halo, "grp", [(0, 1), (1, 0)])
    own_value, own_score, own_max = pl.pallas_call(
        functools.partial(own_kernel, glen),
        out_shape=[
            jax.ShapeDtypeStruct((half, col_count), jnp.bfloat16),
            jax.ShapeDtypeStruct((rows, half), jnp.float32),
            jax.ShapeDtypeStruct((rows, half), jnp.float32),
        ],
        in_specs=[vmem] * 3,
        out_specs=[vmem] * 3,
        compiler_params=params,
        cost_estimate=pl.CostEstimate(flops=3 * 10**8, bytes_accessed=2**20, transcendentals=0),
        name="own_half",
    )(halo, mapped, value_weight)
    return pl.pallas_call(
        halo_kernel,
        out_shape=jax.ShapeDtypeStruct(queries.shape, jnp.bfloat16),
        in_specs=[vmem] * 7 + [hbm],
        out_specs=hbm,
        scratch_shapes=[
            pltpu.VMEM((rows, half), jnp.float32),
            pltpu.VMEM((rows, half), jnp.float32),
            pltpu.VMEM((rows, 2 * half), jnp.bfloat16),
            pltpu.VMEM((glen, col_count), jnp.bfloat16),
            pltpu.SemaphoreType.DMA,
        ],
        input_output_aliases={7: 0},
        compiler_params=params,
        cost_estimate=pl.CostEstimate(flops=10**9, bytes_accessed=4 * 2**20, transcendentals=0),
        name="previous_group",
    )(
        halo_other, own_value, own_score, own_max, mapped, value_weight, edge,
        pltpu.with_memory_space_constraint(out, pltpu.HBM),
    )


def solution(mesh):
    placed = (
        P(None, AXES, "grp"),
        P(None, AXES, None, "grp", None),
        P(None, AXES, None),
        P(None, "grp"),
        P(None, "grp"),
    )
    return jax.shard_map(
        shards,
        mesh=mesh,
        in_specs=placed,
        out_specs=P(None, AXES, "grp"),
        check_vma=False,
    )
```

```python
import math

import jax
import jax.numpy as jnp
from jax import lax
from jax.experimental import pallas as pl
from jax.experimental.pallas import tpu as pltpu
from jax.sharding import PartitionSpec as P

HEAD_DIM = 128
MASK_FILL = -1e30
SCORE_SCALE = HEAD_DIM ** (-0.5) * math.log2(math.e)
DEAD = 8.0
AXES = ("seq", "fsdp")


def dot(a, b):
    return jnp.dot(a, b, preferred_element_type=jnp.float32)


def dot_nt(a, b):
    return lax.dot_general(a, b, (((1,), (1,)), ((), ())), preferred_element_type=jnp.float32)


def softmax_weights(scores, dead):
    scores = jnp.where(dead, MASK_FILL, scores)
    return jnp.exp2(scores - jnp.max(scores, axis=-1, keepdims=True)).astype(jnp.bfloat16)


def mix(weights, rows):
    ones = jnp.ones((rows.shape[0], 128), jnp.bfloat16)
    return dot(weights, jnp.concatenate([rows, ones], axis=1))


def scaled(mixed):
    return mixed[:, :-128] * (1.0 / mixed[:, -1:])


def payload_kernel(length_hbm, enc_hbm, out_ref, length_ref, sems):
    group_count, neighbours, nb_half, _ = enc_hbm.shape[1:]
    rows = [pl.ds(n * nb_half, nb_half) for n in range(neighbours)]
    copies = [
        pltpu.make_async_copy(enc_hbm.at[0, group_count - 1, n], out_ref.at[rows[n]], sems.at[n])
        for n in range(neighbours)
    ]
    lengths = pltpu.make_async_copy(length_hbm, length_ref, sems.at[len(copies)])
    lengths.start()
    for copy in copies:
        copy.start()
    row = lax.broadcasted_iota(jnp.int32, (nb_half, 128), 0) + lax.axis_index("grp") * nb_half
    lane = lax.broadcasted_iota(jnp.int32, (nb_half, 128), 1)
    lengths.wait()
    marks = [(lane == 0) & (row >= length_ref[0, group_count - 1, n]) for n in range(neighbours)]
    for copy in copies:
        copy.wait()
    for n in range(neighbours):
        part = out_ref[rows[n], :128].astype(jnp.float32)
        out_ref[rows[n], :128] = jnp.where(marks[n], DEAD, part).astype(jnp.bfloat16)


def local_kernel(
    length_ref, enc_ref, query_hbm, kw_hbm, vw_hbm, out_hbm, edge_ref, map_ref, query_ref, kw_ref, vw_ref,
    key_ref, value_ref, score_ref, max_ref, weight_ref, out_ref, sems,
):
    tok_count, col_count = query_ref.shape
    head_count = col_count // HEAD_DIM
    neighbours, nb_half, enc_width = enc_ref.shape[3:]
    half = neighbours * nb_half
    glen = tok_count // 2
    heads = [slice(start, start + HEAD_DIM) for start in range(0, col_count, HEAD_DIM)]

    parts = sems.shape[1] - 1
    query_copy = pltpu.make_async_copy(query_hbm.at[0], query_ref, sems.at[0, parts])
    query_copy.start()
    depth = enc_width // parts
    copies = [
        [
            pltpu.make_async_copy(src.at[pl.ds(i * depth, depth)], dst.at[pl.ds(i * depth, depth)], sems.at[j, i])
            for i in range(parts)
        ]
        for j, (src, dst) in enumerate([(kw_hbm, kw_ref), (vw_hbm, vw_ref)])
    ]
    for weight_copies in copies:
        for copy in weight_copies:
            copy.start()

    def group(g):
        rows = [enc_ref[core, 0, g].reshape(half, enc_width) for core in range(2)]
        key = lax.broadcasted_iota(jnp.int32, (1, 2 * half), 1)
        live = key < 0
        for block in range(2 * neighbours):
            first = block * nb_half
            length = jnp.broadcast_to(length_ref[0, g : g + 1, block % neighbours : block % neighbours + 1], key.shape)
            end = first + jnp.clip(length - block // neighbours * nb_half, 0, nb_half)
            live = live | ((key >= first) & (key < end))
        return jnp.concatenate(rows, axis=0), jnp.logical_not(live)

    query_copy.wait()
    query = query_ref[...].astype(jnp.float32)
    row = lax.broadcasted_iota(jnp.int32, (glen, 1), 0)
    halo_query = jnp.where(row < glen - 1, query[:glen], query[tok_count - 1 :]).astype(jnp.bfloat16)
    query = pltpu.roll(query, 1, 0)[glen:].astype(jnp.bfloat16)

    enc, dead = group(0)
    for copy in copies[0]:
        copy.wait()
    key_ref[...] = dot(enc, kw_ref[...]).astype(jnp.bfloat16)

    head_row = lax.broadcasted_iota(jnp.int32, (16, 1), 0)
    lane = lax.broadcasted_iota(jnp.int32, (1, enc_width), 1)
    one_hot = jnp.where(lane == 0, 1.0, 0.0)
    last = jnp.zeros((16, enc_width), jnp.float32)
    for h, cols in enumerate(heads):
        mapped = dot_nt(halo_query[:, cols], kw_ref[:, cols]) * SCORE_SCALE
        last = jnp.where(head_row == h, mapped[glen - 1 :], last)
        map_ref[pl.ds(h * glen, glen), :] = jnp.where(row < glen - 1, mapped, one_hot).astype(jnp.bfloat16)
    for h, cols in enumerate(heads):
        score_ref[pl.ds(h * glen, glen), :] = dot_nt(query[:, cols], key_ref[:, cols]) * SCORE_SCALE

    last_enc, last_dead = group(1)
    last_weights = softmax_weights(dot_nt(last.astype(jnp.bfloat16), last_enc), last_dead)
    last = scaled(mix(last_weights, last_enc)).astype(jnp.bfloat16)

    blocks = [pl.ds(start, 32) for start in range(0, head_count * glen, 32)]
    for block in blocks:
        scores = jnp.where(dead, MASK_FILL, score_ref[block, :])
        max_ref[block, :] = jnp.broadcast_to(jnp.max(scores, axis=-1, keepdims=True), (32, 128))
    for block in blocks:
        top = max_ref[block, :]
        for start in range(0, 2 * half, 128):
            part = slice(start, start + 128)
            scores = jnp.where(dead[:, part], MASK_FILL, score_ref[block, part])
            weight_ref[block, part] = jnp.exp2(scores - top).astype(jnp.bfloat16)

    for copy in copies[1]:
        copy.wait()
    values = dot(jnp.concatenate([enc, last], axis=0), vw_ref[...])
    value_ref[...] = values[: 2 * half].astype(jnp.bfloat16)
    last_out = values[2 * half :]
    token = lax.broadcasted_iota(jnp.int32, (tok_count, 1), 0)
    for h, cols in enumerate(heads):
        out = scaled(mix(weight_ref[pl.ds(h * glen, glen), :], value_ref[:, cols]))
        first = jnp.broadcast_to(last_out[h : h + 1, cols], (glen, HEAD_DIM))
        out = pltpu.roll(jnp.concatenate([first, out], axis=0), tok_count - 1, 0)
        edge_ref[:, cols] = out[glen - 1 : glen]
        out_ref[:, cols] = jnp.where(token < glen - 1, 0.0, out).astype(jnp.bfloat16)
    copy = pltpu.make_async_copy(out_ref, out_hbm.at[0], sems.at[0, 0])
    copy.start()
    copy.wait()


def early_kernel(own_ref, kw_ref, vw_ref, key_ref, value_ref):
    @pl.when(lax.axis_index("grp") == 1)
    def _():
        key_ref[...] = dot(own_ref[...], kw_ref[...]).astype(jnp.bfloat16)
        value_ref[...] = dot(own_ref[...], vw_ref[...]).astype(jnp.bfloat16)


def own_kernel(
    own_ref, query_ref, kw_ref, vw_ref, early_key_ref, early_value_ref, mix_ref, max_ref,
    key_ref, value_ref, score_ref, weight_ref,
):
    own = own_ref[...]
    glen = query_ref.shape[0] // 2
    heads = [slice(start, start + HEAD_DIM) for start in range(0, query_ref.shape[1], HEAD_DIM)]
    blocks = [pl.ds(start, 32) for start in range(0, score_ref.shape[0], 32)]
    early = lax.axis_index("grp") == 1

    @pl.when(early)
    def _():
        key_ref[...] = early_key_ref[...]
        value_ref[...] = early_value_ref[...]

    @pl.when(jnp.logical_not(early))
    def _():
        key_ref[...] = dot(own, kw_ref[...]).astype(jnp.bfloat16)
        value_ref[...] = dot(own, vw_ref[...]).astype(jnp.bfloat16)

    for h, cols in enumerate(heads):
        score_ref[pl.ds(h * glen, glen), :] = dot_nt(query_ref[:glen, cols], key_ref[:, cols]) * SCORE_SCALE
    lane = lax.broadcasted_iota(jnp.int32, (16, 128), 1)
    first_column = dot_nt(jnp.where(lane == 0, 1.0, 0.0).astype(jnp.bfloat16), own[:, :128])
    dead = first_column[0:1] > DEAD - 1.0
    for block in blocks:
        scores = jnp.where(dead, MASK_FILL, score_ref[block, :])
        max_ref[block, :] = jnp.broadcast_to(jnp.max(scores, axis=-1, keepdims=True), scores.shape)
    for block in blocks:
        scores = jnp.where(dead, MASK_FILL, score_ref[block, :])
        weight_ref[block, :] = jnp.exp2(scores - max_ref[block, :]).astype(jnp.bfloat16)
    for h, cols in enumerate(heads):
        rows = pl.ds(h * glen, glen)
        mix_ref[rows, :] = mix(weight_ref[rows, :], value_ref[:, cols])


def halo_kernel(
    other_ref, own_mix_ref, own_max_ref, map_ref, vw_ref, edge_ref, _, out_hbm,
    value_ref, score_ref, own_scale_ref, weight_ref, top_ref, sem,
):
    glen, col_count = top_ref.shape
    row_count, half = score_ref.shape
    heads = [slice(start, start + HEAD_DIM) for start in range(0, col_count, HEAD_DIM)]
    blocks = [pl.ds(start, 32) for start in range(0, row_count, 32)]

    @pl.when(lax.axis_index(AXES) > 0)
    def _():
        other = other_ref[...]
        score_ref[...] = dot_nt(map_ref[...], other)
        value_ref[...] = dot(other, vw_ref[...]).astype(jnp.bfloat16)
        dead = score_ref[glen - 1 : glen, :] > DEAD - 1.0
        for block in blocks:
            scores = jnp.where(dead, MASK_FILL, score_ref[block, :])
            own_max = own_max_ref[block, :]
            top = jnp.maximum(own_max, jnp.max(scores, axis=-1, keepdims=True))
            own_scale_ref[block, :] = jnp.exp2(own_max - top)
            weight_ref[block, :] = jnp.exp2(scores - top).astype(jnp.bfloat16)
        row = lax.broadcasted_iota(jnp.int32, (glen, 1), 0)
        for h, cols in enumerate(heads):
            rows = pl.ds(h * glen, glen)
            mixed = mix(weight_ref[rows, :], value_ref[:, cols])
            scale = own_scale_ref[rows, :]
            total = own_mix_ref[rows, HEAD_DIM:] * scale + mixed[:, HEAD_DIM:]
            out = (own_mix_ref[rows, :HEAD_DIM] * scale + mixed[:, :HEAD_DIM]) * (1.0 / total)
            top_ref[:, cols] = jnp.where(row < glen - 1, out, edge_ref[:, cols]).astype(jnp.bfloat16)
        copy = pltpu.make_async_copy(top_ref, out_hbm.at[0, pl.ds(0, glen)], sem)
        copy.start()
        copy.wait()


def shards(queries, encodings, neighbour_lengths, key_weight, value_weight):
    tok_count, col_count = queries.shape[1:]
    group_count, neighbours, nb_half, enc_width = encodings.shape[1:]
    half = neighbours * nb_half
    glen = tok_count // group_count
    rows = col_count // HEAD_DIM * glen
    vmem = pl.BlockSpec(memory_space=pltpu.VMEM)
    hbm = pl.BlockSpec(memory_space=pltpu.HBM)
    params = pltpu.CompilerParams(vmem_limit_bytes=24 * 2**20)

    payload = pl.pallas_call(
        payload_kernel,
        out_shape=pltpu.VMEM((half, enc_width), jnp.bfloat16),
        in_specs=[hbm, hbm],
        out_specs=vmem,
        scratch_shapes=[pltpu.SMEM(neighbour_lengths.shape, jnp.int32), pltpu.SemaphoreType.DMA((neighbours + 1,))],
        compiler_params=pltpu.CompilerParams(vmem_limit_bytes=127 * 2**19),
        cost_estimate=pl.CostEstimate(flops=10**10, bytes_accessed=2**20, transcendentals=0),
        name="payload",
    )(*(pltpu.with_memory_space_constraint(x, pltpu.HBM) for x in (neighbour_lengths, encodings)))
    size = lax.axis_size(AXES)
    halo = lax.ppermute(payload, AXES, [(i, (i + 1) % size) for i in range(size)])
    enc = lax.all_gather(encodings, "grp", axis=0)
    fetched = (pltpu.with_memory_space_constraint(x, pltpu.HBM) for x in (queries, key_weight, value_weight))
    out, edge, mapped, queries, key_weight, value_weight = pl.pallas_call(
        local_kernel,
        out_shape=[
            jax.ShapeDtypeStruct(queries.shape, jnp.bfloat16),
            jax.ShapeDtypeStruct((1, col_count), jnp.float32),
            jax.ShapeDtypeStruct((rows, enc_width), jnp.bfloat16),
            jax.ShapeDtypeStruct((tok_count, col_count), jnp.bfloat16),
            jax.ShapeDtypeStruct(key_weight.shape, jnp.bfloat16),
            jax.ShapeDtypeStruct(value_weight.shape, jnp.bfloat16),
        ],
        in_specs=[vmem] * 2 + [hbm] * 3,
        out_specs=[hbm] + [vmem] * 5,
        scratch_shapes=[
            pltpu.VMEM((2 * half, col_count), jnp.bfloat16),
            pltpu.VMEM((2 * half, col_count), jnp.bfloat16),
            pltpu.VMEM((rows, 2 * half), jnp.float32),
            pltpu.VMEM((rows, 128), jnp.float32),
            pltpu.VMEM((rows, 2 * half), jnp.bfloat16),
            pltpu.VMEM((tok_count, col_count), jnp.bfloat16),
            pltpu.SemaphoreType.DMA((2, 5)),
        ],
        compiler_params=params,
        cost_estimate=pl.CostEstimate(flops=2 * 10**9, bytes_accessed=6 * 2**20, transcendentals=0),
        name="local_groups",
    )(neighbour_lengths, enc, *fetched)

    halo, out, queries = lax.optimization_barrier((halo, out, queries))
    early = pl.pallas_call(
        early_kernel,
        out_shape=[jax.ShapeDtypeStruct((half, col_count), jnp.bfloat16)] * 2,
        in_specs=[vmem] * 3,
        out_specs=[vmem] * 2,
        compiler_params=params,
        cost_estimate=pl.CostEstimate(flops=5 * 10**8, bytes_accessed=2**20, transcendentals=0),
        name="early_half",
    )(halo, key_weight, value_weight)
    halo, early = lax.optimization_barrier((halo, early))
    halo_other = lax.ppermute(halo, "grp", [(0, 1), (1, 0)])
    own_mix, own_max = pl.pallas_call(
        own_kernel,
        out_shape=[
            jax.ShapeDtypeStruct((rows, HEAD_DIM + 128), jnp.float32),
            jax.ShapeDtypeStruct((rows, half), jnp.float32),
        ],
        in_specs=[vmem] * 6,
        out_specs=[vmem] * 2,
        scratch_shapes=[
            pltpu.VMEM((half, col_count), jnp.bfloat16),
            pltpu.VMEM((half, col_count), jnp.bfloat16),
            pltpu.VMEM((rows, half), jnp.float32),
            pltpu.VMEM((rows, half), jnp.bfloat16),
        ],
        compiler_params=params,
        cost_estimate=pl.CostEstimate(flops=5 * 10**8, bytes_accessed=2**20, transcendentals=0),
        name="own_half",
    )(halo, queries, key_weight, value_weight, *early)
    return pl.pallas_call(
        halo_kernel,
        out_shape=jax.ShapeDtypeStruct(out.shape, jnp.bfloat16),
        in_specs=[vmem] * 6 + [hbm],
        out_specs=hbm,
        scratch_shapes=[
            pltpu.VMEM((half, col_count), jnp.bfloat16),
            pltpu.VMEM((rows, half), jnp.float32),
            pltpu.VMEM((rows, half), jnp.float32),
            pltpu.VMEM((rows, half), jnp.bfloat16),
            pltpu.VMEM((glen, col_count), jnp.bfloat16),
            pltpu.SemaphoreType.DMA,
        ],
        input_output_aliases={6: 0},
        compiler_params=params,
        cost_estimate=pl.CostEstimate(flops=10**9, bytes_accessed=4 * 2**20, transcendentals=0),
        name="previous_group",
    )(
        halo_other, own_mix, own_max, mapped, value_weight, edge,
        pltpu.with_memory_space_constraint(out, pltpu.HBM),
    )


def solution(mesh):
    placed = (
        P(None, AXES, "grp"),
        P(None, AXES, None, "grp", None),
        P(None, AXES, None),
        P(None, "grp"),
        P(None, "grp"),
    )
    return jax.shard_map(
        shards,
        mesh=mesh,
        in_specs=placed,
        out_specs=P(None, AXES, "grp"),
        check_vma=False,
    )
```

```python
import math

import jax
import jax.numpy as jnp
from jax import lax
from jax.experimental import pallas as pl
from jax.experimental.pallas import tpu as pltpu
from jax.sharding import PartitionSpec as P

HEAD_DIM = 128
MASK_FILL = -1e30
SCORE_SCALE = HEAD_DIM ** (-0.5) * math.log2(math.e)
DEAD = 8.0
AXES = ("seq", "fsdp")


def dot(a, b):
    return jnp.dot(a, b, preferred_element_type=jnp.float32)


def dot_nt(a, b):
    return lax.dot_general(a, b, (((1,), (1,)), ((), ())), preferred_element_type=jnp.float32)


def softmax_weights(scores, dead):
    scores = jnp.where(dead, MASK_FILL, scores)
    return jnp.exp2(scores - jnp.max(scores, axis=-1, keepdims=True)).astype(jnp.bfloat16)


def mix(weights, rows):
    ones = jnp.ones((rows.shape[0], 128), jnp.bfloat16)
    return dot(weights, jnp.concatenate([rows, ones], axis=1))


def scaled(mixed):
    return mixed[:, :-128] * (1.0 / mixed[:, -1:])


def payload_kernel(length_hbm, enc_hbm, out_ref, length_ref, sems):
    group_count, neighbours, nb_half, _ = enc_hbm.shape[1:]
    rows = [pl.ds(n * nb_half, nb_half) for n in range(neighbours)]
    part = nb_half // 2
    copies = [
        pltpu.make_async_copy(
            enc_hbm.at[0, group_count - 1, n, pl.ds(i * part, part)],
            out_ref.at[pl.ds(n * nb_half + i * part, part)],
            sems.at[2 * n + i],
        )
        for n in range(neighbours)
        for i in range(2)
    ]
    lengths = pltpu.make_async_copy(length_hbm, length_ref, sems.at[len(copies)])
    for copy in copies + [lengths]:
        copy.start()
    row = lax.broadcasted_iota(jnp.int32, (nb_half, 128), 0) + lax.axis_index("grp") * nb_half
    lane = lax.broadcasted_iota(jnp.int32, (nb_half, 128), 1)
    lengths.wait()
    marks = [(lane == 0) & (row >= length_ref[0, group_count - 1, n]) for n in range(neighbours)]
    for copy in copies:
        copy.wait()
    for n in range(neighbours):
        marked = jnp.where(marks[n], DEAD, out_ref[rows[n], :128].astype(jnp.float32))
        out_ref[rows[n], :128] = marked.astype(jnp.bfloat16)


def local_kernel(
    length_ref, enc_ref, query_hbm, kw_hbm, vw_hbm, out_hbm, edge_ref, map_ref, query_ref, kw_ref, vw_ref,
    key_ref, value_ref, score_ref, max_ref, weight_ref, out_ref, sems,
):
    tok_count, col_count = query_ref.shape
    head_count = col_count // HEAD_DIM
    neighbours, nb_half, enc_width = enc_ref.shape[3:]
    half = neighbours * nb_half
    glen = tok_count // 2
    heads = [slice(start, start + HEAD_DIM) for start in range(0, col_count, HEAD_DIM)]

    parts = sems.shape[1] - 1
    query_copy = pltpu.make_async_copy(query_hbm.at[0], query_ref, sems.at[0, parts])
    query_copy.start()
    depth = enc_width // parts
    copies = [
        [
            pltpu.make_async_copy(src.at[pl.ds(i * depth, depth)], dst.at[pl.ds(i * depth, depth)], sems.at[j, i])
            for i in range(parts)
        ]
        for j, (src, dst) in enumerate([(kw_hbm, kw_ref), (vw_hbm, vw_ref)])
    ]
    for weight_copies in copies:
        for copy in weight_copies:
            copy.start()

    def group(g):
        rows = [enc_ref[core, 0, g].reshape(half, enc_width) for core in range(2)]
        key = lax.broadcasted_iota(jnp.int32, (1, 2 * half), 1)
        live = key < 0
        for block in range(2 * neighbours):
            first = block * nb_half
            length = jnp.broadcast_to(length_ref[0, g : g + 1, block % neighbours : block % neighbours + 1], key.shape)
            end = first + jnp.clip(length - block // neighbours * nb_half, 0, nb_half)
            live = live | ((key >= first) & (key < end))
        return jnp.concatenate(rows, axis=0), jnp.logical_not(live)

    query_copy.wait()
    query = query_ref[...].astype(jnp.float32)
    row = lax.broadcasted_iota(jnp.int32, (glen, 1), 0)
    halo_query = jnp.where(row < glen - 1, query[:glen], query[tok_count - 1 :]).astype(jnp.bfloat16)
    query = pltpu.roll(query, 1, 0)[glen:].astype(jnp.bfloat16)

    enc, dead = group(0)
    for copy in copies[0]:
        copy.wait()
    key_ref[...] = dot(enc, kw_ref[...]).astype(jnp.bfloat16)

    head_row = lax.broadcasted_iota(jnp.int32, (16, 1), 0)
    lane = lax.broadcasted_iota(jnp.int32, (1, enc_width), 1)
    one_hot = jnp.where(lane == 0, 1.0, 0.0)
    last = jnp.zeros((16, enc_width), jnp.float32)
    for h, cols in enumerate(heads):
        mapped = dot_nt(halo_query[:, cols], kw_ref[:, cols]) * SCORE_SCALE
        last = jnp.where(head_row == h, mapped[glen - 1 :], last)
        map_ref[pl.ds(h * glen, glen), :] = jnp.where(row < glen - 1, mapped, one_hot).astype(jnp.bfloat16)
    for h, cols in enumerate(heads):
        score_ref[pl.ds(h * glen, glen), :] = dot_nt(query[:, cols], key_ref[:, cols]) * SCORE_SCALE

    last_enc, last_dead = group(1)
    last_weights = softmax_weights(dot_nt(last.astype(jnp.bfloat16), last_enc), last_dead)
    last = scaled(mix(last_weights, last_enc)).astype(jnp.bfloat16)

    blocks = [pl.ds(start, 32) for start in range(0, head_count * glen, 32)]
    for block in blocks:
        scores = jnp.where(dead, MASK_FILL, score_ref[block, :])
        max_ref[block, :] = jnp.broadcast_to(jnp.max(scores, axis=-1, keepdims=True), (32, 128))
    for block in blocks:
        top = max_ref[block, :]
        for start in range(0, 2 * half, 128):
            part = slice(start, start + 128)
            scores = jnp.where(dead[:, part], MASK_FILL, score_ref[block, part])
            weight_ref[block, part] = jnp.exp2(scores - top).astype(jnp.bfloat16)

    for copy in copies[1]:
        copy.wait()
    values = dot(jnp.concatenate([enc, last], axis=0), vw_ref[...])
    value_ref[...] = values[: 2 * half].astype(jnp.bfloat16)
    last_out = values[2 * half :]
    token = lax.broadcasted_iota(jnp.int32, (tok_count, 1), 0)
    for h, cols in enumerate(heads):
        out = scaled(mix(weight_ref[pl.ds(h * glen, glen), :], value_ref[:, cols]))
        first = jnp.broadcast_to(last_out[h : h + 1, cols], (glen, HEAD_DIM))
        out = pltpu.roll(jnp.concatenate([first, out], axis=0), tok_count - 1, 0)
        edge_ref[:, cols] = out[glen - 1 : glen]
        out_ref[:, cols] = jnp.where(token < glen - 1, 0.0, out).astype(jnp.bfloat16)
    copy = pltpu.make_async_copy(out_ref, out_hbm.at[0], sems.at[0, 0])
    copy.start()
    copy.wait()


def early_kernel(own_ref, kw_ref, vw_ref, key_ref, value_ref):
    @pl.when(lax.axis_index("grp") == 1)
    def _():
        key_ref[...] = dot(own_ref[...], kw_ref[...]).astype(jnp.bfloat16)
        value_ref[...] = dot(own_ref[...], vw_ref[...]).astype(jnp.bfloat16)


def own_kernel(
    own_ref, query_ref, kw_ref, vw_ref, early_key_ref, early_value_ref, mix_ref, max_ref,
    key_ref, value_ref, score_ref, weight_ref,
):
    own = own_ref[...]
    glen = query_ref.shape[0] // 2
    heads = [slice(start, start + HEAD_DIM) for start in range(0, query_ref.shape[1], HEAD_DIM)]
    blocks = [pl.ds(start, 32) for start in range(0, score_ref.shape[0], 32)]
    early = lax.axis_index("grp") == 1

    @pl.when(early)
    def _():
        key_ref[...] = early_key_ref[...]
        value_ref[...] = early_value_ref[...]

    @pl.when(jnp.logical_not(early))
    def _():
        key_ref[...] = dot(own, kw_ref[...]).astype(jnp.bfloat16)
        value_ref[...] = dot(own, vw_ref[...]).astype(jnp.bfloat16)

    for h, cols in enumerate(heads):
        score_ref[pl.ds(h * glen, glen), :] = dot_nt(query_ref[:glen, cols], key_ref[:, cols]) * SCORE_SCALE
    lane = lax.broadcasted_iota(jnp.int32, (16, 128), 1)
    first_column = dot_nt(jnp.where(lane == 0, 1.0, 0.0).astype(jnp.bfloat16), own[:, :128])
    dead = first_column[0:1] > DEAD - 1.0
    for block in blocks:
        scores = jnp.where(dead, MASK_FILL, score_ref[block, :])
        max_ref[block, :] = jnp.broadcast_to(jnp.max(scores, axis=-1, keepdims=True), scores.shape)
    for block in blocks:
        scores = jnp.where(dead, MASK_FILL, score_ref[block, :])
        weight_ref[block, :] = jnp.exp2(scores - max_ref[block, :]).astype(jnp.bfloat16)
    for h, cols in enumerate(heads):
        rows = pl.ds(h * glen, glen)
        mix_ref[rows, :] = mix(weight_ref[rows, :], value_ref[:, cols])


def halo_kernel(
    other_ref, own_mix_ref, own_max_ref, map_ref, vw_ref, edge_ref, _, out_hbm,
    value_ref, score_ref, max_ref, own_scale_ref, weight_ref, mix_ref, top_ref, sem,
):
    glen, col_count = top_ref.shape
    row_count, half = score_ref.shape
    heads = [slice(start, start + HEAD_DIM) for start in range(0, col_count, HEAD_DIM)]
    blocks = [pl.ds(start, 32) for start in range(0, row_count, 32)]

    @pl.when(lax.axis_index(AXES) > 0)
    def _():
        other = other_ref[...]
        score_ref[...] = dot_nt(map_ref[...], other)
        value_ref[...] = dot(other, vw_ref[...]).astype(jnp.bfloat16)
        dead = score_ref[glen - 1 : glen, :] > DEAD - 1.0
        for block in blocks:
            scores = jnp.where(dead, MASK_FILL, score_ref[block, :])
            own_max = own_max_ref[block, :]
            top = jnp.maximum(own_max, jnp.max(scores, axis=-1, keepdims=True))
            max_ref[block, :] = top
        for block in blocks:
            top = max_ref[block, :]
            own_scale_ref[block, :] = jnp.exp2(own_max_ref[block, :] - top)
            scores = jnp.where(dead, MASK_FILL, score_ref[block, :])
            weight_ref[block, :] = jnp.exp2(scores - top).astype(jnp.bfloat16)
        for h, cols in enumerate(heads):
            rows = pl.ds(h * glen, glen)
            mix_ref[rows, :] = mix(weight_ref[rows, :], value_ref[:, cols])
        row = lax.broadcasted_iota(jnp.int32, (glen, 1), 0)
        for h, cols in enumerate(heads):
            rows = pl.ds(h * glen, glen)
            scale = own_scale_ref[rows, :]
            total = own_mix_ref[rows, HEAD_DIM:] * scale + mix_ref[rows, HEAD_DIM:]
            out = (own_mix_ref[rows, :HEAD_DIM] * scale + mix_ref[rows, :HEAD_DIM]) * (1.0 / total)
            top_ref[:, cols] = jnp.where(row < glen - 1, out, edge_ref[:, cols]).astype(jnp.bfloat16)
        copy = pltpu.make_async_copy(top_ref, out_hbm.at[0, pl.ds(0, glen)], sem)
        copy.start()
        copy.wait()


def shards(queries, encodings, neighbour_lengths, key_weight, value_weight):
    tok_count, col_count = queries.shape[1:]
    group_count, neighbours, nb_half, enc_width = encodings.shape[1:]
    half = neighbours * nb_half
    glen = tok_count // group_count
    rows = col_count // HEAD_DIM * glen
    vmem = pl.BlockSpec(memory_space=pltpu.VMEM)
    hbm = pl.BlockSpec(memory_space=pltpu.HBM)
    params = pltpu.CompilerParams(vmem_limit_bytes=24 * 2**20)

    payload = pl.pallas_call(
        payload_kernel,
        out_shape=pltpu.VMEM((half, enc_width), jnp.bfloat16),
        in_specs=[hbm, hbm],
        out_specs=vmem,
        scratch_shapes=[pltpu.SMEM(neighbour_lengths.shape, jnp.int32), pltpu.SemaphoreType.DMA((2 * neighbours + 1,))],
        compiler_params=pltpu.CompilerParams(vmem_limit_bytes=127 * 2**19),
        cost_estimate=pl.CostEstimate(flops=10**10, bytes_accessed=2**20, transcendentals=0),
        name="payload",
    )(*(pltpu.with_memory_space_constraint(x, pltpu.HBM) for x in (neighbour_lengths, encodings)))
    size = lax.axis_size(AXES)
    halo = lax.ppermute(payload, AXES, [(i, (i + 1) % size) for i in range(size)])
    enc = lax.all_gather(encodings, "grp", axis=0)
    fetched = (pltpu.with_memory_space_constraint(x, pltpu.HBM) for x in (queries, key_weight, value_weight))
    out, edge, mapped, queries, key_weight, value_weight = pl.pallas_call(
        local_kernel,
        out_shape=[
            jax.ShapeDtypeStruct(queries.shape, jnp.bfloat16),
            jax.ShapeDtypeStruct((1, col_count), jnp.float32),
            jax.ShapeDtypeStruct((rows, enc_width), jnp.bfloat16),
            jax.ShapeDtypeStruct((tok_count, col_count), jnp.bfloat16),
            jax.ShapeDtypeStruct(key_weight.shape, jnp.bfloat16),
            jax.ShapeDtypeStruct(value_weight.shape, jnp.bfloat16),
        ],
        in_specs=[vmem] * 2 + [hbm] * 3,
        out_specs=[hbm] + [vmem] * 5,
        scratch_shapes=[
            pltpu.VMEM((2 * half, col_count), jnp.bfloat16),
            pltpu.VMEM((2 * half, col_count), jnp.bfloat16),
            pltpu.VMEM((rows, 2 * half), jnp.float32),
            pltpu.VMEM((rows, 128), jnp.float32),
            pltpu.VMEM((rows, 2 * half), jnp.bfloat16),
            pltpu.VMEM((tok_count, col_count), jnp.bfloat16),
            pltpu.SemaphoreType.DMA((2, 5)),
        ],
        compiler_params=params,
        cost_estimate=pl.CostEstimate(flops=2 * 10**9, bytes_accessed=6 * 2**20, transcendentals=0),
        name="local_groups",
    )(neighbour_lengths, enc, *fetched)

    halo, out, queries = lax.optimization_barrier((halo, out, queries))
    early = pl.pallas_call(
        early_kernel,
        out_shape=[jax.ShapeDtypeStruct((half, col_count), jnp.bfloat16)] * 2,
        in_specs=[vmem] * 3,
        out_specs=[vmem] * 2,
        compiler_params=params,
        cost_estimate=pl.CostEstimate(flops=5 * 10**8, bytes_accessed=2**20, transcendentals=0),
        name="early_half",
    )(halo, key_weight, value_weight)
    halo, early = lax.optimization_barrier((halo, early))
    halo_other = lax.ppermute(halo, "grp", [(0, 1), (1, 0)])
    own_mix, own_max = pl.pallas_call(
        own_kernel,
        out_shape=[
            jax.ShapeDtypeStruct((rows, HEAD_DIM + 128), jnp.float32),
            jax.ShapeDtypeStruct((rows, half), jnp.float32),
        ],
        in_specs=[vmem] * 6,
        out_specs=[vmem] * 2,
        scratch_shapes=[
            pltpu.VMEM((half, col_count), jnp.bfloat16),
            pltpu.VMEM((half, col_count), jnp.bfloat16),
            pltpu.VMEM((rows, half), jnp.float32),
            pltpu.VMEM((rows, half), jnp.bfloat16),
        ],
        compiler_params=params,
        cost_estimate=pl.CostEstimate(flops=5 * 10**8, bytes_accessed=2**20, transcendentals=0),
        name="own_half",
    )(halo, queries, key_weight, value_weight, *early)
    return pl.pallas_call(
        halo_kernel,
        out_shape=jax.ShapeDtypeStruct(out.shape, jnp.bfloat16),
        in_specs=[vmem] * 6 + [hbm],
        out_specs=hbm,
        scratch_shapes=[
            pltpu.VMEM((half, col_count), jnp.bfloat16),
            pltpu.VMEM((rows, half), jnp.float32),
            pltpu.VMEM((rows, half), jnp.float32),
            pltpu.VMEM((rows, half), jnp.float32),
            pltpu.VMEM((rows, half), jnp.bfloat16),
            pltpu.VMEM((rows, HEAD_DIM + 128), jnp.float32),
            pltpu.VMEM((glen, col_count), jnp.bfloat16),
            pltpu.SemaphoreType.DMA,
        ],
        input_output_aliases={6: 0},
        compiler_params=params,
        cost_estimate=pl.CostEstimate(flops=10**9, bytes_accessed=4 * 2**20, transcendentals=0),
        name="previous_group",
    )(
        halo_other, own_mix, own_max, mapped, value_weight, edge,
        pltpu.with_memory_space_constraint(out, pltpu.HBM),
    )


def solution(mesh):
    placed = (
        P(None, AXES, "grp"),
        P(None, AXES, None, "grp", None),
        P(None, AXES, None),
        P(None, "grp"),
        P(None, "grp"),
    )
    return jax.shard_map(
        shards,
        mesh=mesh,
        in_specs=placed,
        out_specs=P(None, AXES, "grp"),
        check_vma=False,
    )
```
